256 devices in a mesh: bins: 32 (over x, z), samp: 8 (over y, core).
Axes of the slice: x: 4, y: 4, z: 8, core: 2. Of those that a mesh axis runs over, the one named last changes fastest.
Arguments:
- signal: float32 [2048, 32768], P('samp', 'bins'), may hold values from -6 to 6
- jumps: float32 [2048, 1024], P('samp', 'bins'), as said below
- breaks: int32 [1024], P('bins'), may hold values from 0 to 32766, as said below
Outputs:
- residual: float32 [2048, 32768], P('samp', 'bins')
- jumps_out: float32 [2048, 1024], P('samp', 'bins')
The draws below stay inside these ranges and needn't reach their ends.
Inputs may be any that keep to these rules, and one draw needn't show every extreme that they name: Entries 32 * d to 32 * (d + 1) - 1 of breaks lie in bins d * 1024 to (d + 1) * 1024 - 2; entries may repeat; the first breakpoint is at bin 0 and the last at bin 32768 - 2. `jumps`: jumps of different breakpoints have different scales.
All inputs are finite; a program needn't handle non-finite values.
Results may differ from the reference program's by a relative error of at most 0.00011.
Values sent between devices are 32-bit elements; how exact they have to be, the bound alone decides.
No kernel may reach another device: no remote copies, remote signals or barrier semaphores. Data moves between devices by JAX's collectives and lax.ppermute only.
A program may use at most 64 MiB of HBM per device.

```python
import math
import jax
import jax.numpy as jnp
from jax import lax

BIN_DEV = 1024
K_DEV = 32
PASSES = 2
S = 2048
NB = 32768
K = 1024


def draw_jumps(key, part):
    key = jax.random.fold_in(key, 11)
    key_scale, key_base = jax.random.split(key, 2)
    col_scale = jnp.exp(jax.random.uniform(key_scale, (1, K), jnp.float32, math.log(0.01), math.log(0.2)))
    base = jax.random.normal(key_base, (S, K), jnp.float32)
    return (base * col_scale).astype(jnp.float32)


def draw_breaks(key, part):
    key = jax.random.fold_in(key, 23)
    offsets = jax.random.randint(key, (K,), 0, BIN_DEV - 1, jnp.int32)
    position = jnp.arange(K, dtype=jnp.int32)
    offsets = jnp.where(position == 0, 0, offsets)
    offsets = jnp.where(position == K - 1, BIN_DEV - 2, offsets)
    blocks = position // K_DEV
    return (blocks * BIN_DEV + offsets).astype(jnp.int32)


def shard_levels(key, shape, pieces, smallest, top_value):
    def one(dim, shards_of):
        heights = jax.random.uniform(jax.random.fold_in(jax.random.fold_in(key, 6), dim), (shards_of,), jnp.float32, smallest / len(pieces), top_value / len(pieces))
        return jnp.repeat(jnp.exp(heights), shape[dim] // shards_of).reshape((-1,) + (1,) * (len(shape) - dim - 1))

    level = one(*pieces[0])
    for cut in pieces[1:]:
        level = level * one(*cut)
    return level


def noise(key, extent, spread, limit, cuts=(), kind=jnp.bfloat16):
    drawn = spread * jax.random.normal(key, extent, jnp.float32)
    if cuts:
        drawn = drawn * shard_levels(key, extent, cuts, -0.22, 0.18)
    return jnp.clip(drawn, -limit, limit).astype(kind)


def setup_inputs(seed: int = 0) -> dict:
    splits = jax.random.split(jax.random.key(seed), 4)
    return {
        "signal": noise(splits[0], (S, NB), 1.0, 6.0, ((0, 8), (1, 32)), jnp.float32),
        "jumps": draw_jumps(jax.random.fold_in(splits[3], 71), 0),
        "breaks": draw_breaks(jax.random.fold_in(splits[3], 71), 0),
    }


epsilon = 1e-06
shrink_level = 0.5

def steps_of(amounts, breaks):
    jump_field = jnp.zeros((S, NB), jnp.float32).at[:, breaks].add(amounts)
    return jnp.cumsum(jump_field, axis=1) - jump_field

def correlate(resid, breaks):
    inclusive = jnp.cumsum(resid, axis=1)
    return inclusive[:, -1:] - inclusive[:, breaks]

def reference(signal, jumps, breaks):
    resid = signal - steps_of(jumps, breaks)
    for step_num in range(PASSES):
        corr = correlate(resid, breaks)
        grad_sum = jnp.sum(corr * corr)
        image = steps_of(corr, breaks)
        curv_sum = jnp.sum(image * image)
        step_size = grad_sum / (curv_sum + epsilon)
        moved = jumps + step_size * corr
        group_norm = jnp.sqrt(lax.optimization_barrier(jnp.sum(moved * moved, axis=0)) + epsilon)
        level_mean = jnp.mean(group_norm)
        shrunk = moved * jnp.maximum(0.0, 1.0 - shrink_level * level_mean / group_norm)
        resid = resid - steps_of(shrunk - jumps, breaks)
        jumps = shrunk
    return (resid, jumps)
```

```python
import functools

import jax
import jax.numpy as jnp
from jax import lax
from jax.experimental import pallas as pl
from jax.experimental.pallas import tpu as pltpu
from jax.sharding import Mesh, PartitionSpec as P

EPS = 1e-06
SHRINK = 0.5
NX, NZ, NY, NC = 4, 8, 4, 2
KD = 32
KZ = KD * NZ
F32 = jnp.float32
BF16 = jnp.bfloat16
VMEM = pl.BlockSpec(memory_space=pltpu.VMEM)
SMEM = pl.BlockSpec(memory_space=pltpu.SMEM)


def pieces(v):
    hi = v.astype(BF16)
    rest = v - hi.astype(F32)
    mid = rest.astype(BF16)
    low = (rest - mid.astype(F32)).astype(BF16)
    return hi, mid, low


def dot(a, b):
    return jnp.dot(a, b, precision=lax.Precision.HIGHEST, preferred_element_type=F32)


def call(kernel, out_shape, n_in, smem=0, limit=32):
    n_out = len(out_shape)
    return pl.pallas_call(
        kernel,
        out_shape=[jax.ShapeDtypeStruct(s, F32) for s in out_shape],
        in_specs=[SMEM] * smem + [VMEM] * (n_in - smem),
        out_specs=[VMEM] * n_out,
        compiler_params=pltpu.CompilerParams(vmem_limit_bytes=limit << 20),
    )


def local_sums(breaks, signal, jumps, out):
    rows, width = signal.shape
    z = lax.axis_index("z")
    start = (lax.axis_index("x") * NZ + z) * width
    sub = lax.broadcasted_iota(jnp.int32, (40, 128), 0)
    lane = lax.broadcasted_iota(jnp.int32, (8, KZ), 1)
    at = jnp.where(sub == KD, -1, width)
    row = jnp.zeros((8, KZ), jnp.int32)
    for k in range(KD):
        at = jnp.where(sub == k, breaks[k] - start, at)
        row = jnp.where(lane == z * KD + k, breaks[k], row)
    at = jnp.concatenate([at] * (width // 128), axis=1)
    mask = (lax.broadcasted_iota(jnp.int32, (40, width), 1) > at).astype(BF16)
    total = jnp.zeros((40, rows), F32)
    for piece in pieces(signal[...])[::-1]:
        total += lax.dot_general(mask, piece, (((1,), (1,)), ((), ())), preferred_element_type=F32)
    out[0:KD, :] = jumps[...].T
    out[KD : 2 * KD, :] = total[:KD]
    sub8 = lax.broadcasted_iota(jnp.int32, (8, KZ), 0)
    out[2 * KD :, :] = jnp.where(sub8 == 1, row.astype(F32), total[KD:])


def gram(after):
    wide = jnp.broadcast_to(after, (KZ, KZ))
    return jnp.minimum(wide, wide.T), wide


def group_sums(bins, got, out):
    head = got[...]
    marks = jnp.sum(head[:, 2 * KD + 1, :], axis=0, keepdims=True)
    after = (bins - 1.0) - marks
    overlap, wide = gram(after)
    jumps = head[:, :KD, :].reshape(KZ, KZ)
    later = jnp.zeros((1, KZ), F32)
    behind = [None] * NZ
    for z in range(NZ - 1, -1, -1):
        behind[z] = head[z, KD : 2 * KD, :] + later
        later = later + head[z, 2 * KD : 2 * KD + 1, :]
    corr = jnp.concatenate(behind, axis=0) - dot(overlap, jumps)
    out[0:KZ, :] = jumps.T
    out[KZ : 2 * KZ, :] = corr.T
    out[2 * KZ : 2 * KZ + 1, :] = later
    out[2 * KZ + 1 : 2 * KZ + 2, :] = jnp.sum(jumps, axis=0, keepdims=True)
    out[2 * KZ + 2 : 2 * KZ + 3, :] = jnp.sum(jumps * wide.T, axis=0, keepdims=True)
    out[2 * KZ + 3 : 2 * KZ + 4, :] = after
    out[2 * KZ + 4 :, :] = jnp.zeros((4, KZ), F32)


def places():
    x = lax.axis_index("x")
    return [lax.rem(x + NX - k, NX) for k in range(NX)]


def carries(place, lower, upper):
    before, behind = [], []
    for p in range(NX):
        a, b = 0.0, 0.0
        for q in range(NX):
            if q != p:
                a = a + jnp.where(place[q] < place[p], lower[q], 0.0)
                b = b + jnp.where(place[q] > place[p], upper[q], 0.0)
        before.append(a)
        behind.append(b)
    return before, behind


def write_stats(stats, place, jumps, corr, after, overlap):
    sums, weighted = [], []
    for p in range(NX):
        c, j = corr[p], jumps[p]
        sums.append(jnp.sum(c, axis=1, keepdims=True))
        weighted.append(jnp.sum(c * after[p], axis=1, keepdims=True))
        stats[3 * p : 3 * p + 1, :] = jnp.sum(j * j, axis=0, keepdims=True)
        stats[3 * p + 1 : 3 * p + 2, :] = jnp.sum(j * c, axis=0, keepdims=True)
        stats[3 * p + 2 : 3 * p + 3, :] = jnp.sum(c * c, axis=0, keepdims=True)
    before, _ = carries(place, sums, weighted)
    curv = jnp.zeros((1, KZ), F32)
    cross = jnp.zeros((KZ, 1), F32)
    for p in range(NX):
        curv += jnp.sum(corr[p] * dot(corr[p], overlap[p]), axis=0, keepdims=True)
        cross += weighted[p] * before[p]
    lane = lax.broadcasted_iota(jnp.int32, (1, KZ), 1)
    curv += jnp.where(lane == 0, 2.0 * jnp.sum(cross), 0.0)
    stats[3 * NX : 3 * NX + 1, :] = curv
    stats[3 * NX + 1 :, :] = jnp.zeros((3, KZ), F32)


def first_corr(g0, g1, g2, g3, corr_out, stats):
    place = places()
    groups = (g0, g1, g2, g3)
    row = lambda p, k: groups[p][2 * KZ + k : 2 * KZ + k + 1, :]
    after = [row(p, 3) for p in range(NX)]
    overlap = [gram(a)[0] for a in after]
    before, behind = carries(place, [row(p, 1) for p in range(NX)], [row(p, 0) - row(p, 2) for p in range(NX)])
    columns = jnp.concatenate(before + behind, axis=0).T
    corr = []
    for p in range(NX):
        c = groups[p][KZ : 2 * KZ, :] + columns[:, NX + p : NX + p + 1] - columns[:, p : p + 1] * after[p]
        corr_out[p] = c
        corr.append(c)
    write_stats(stats, place, [g[0:KZ, :] for g in groups], corr, after, overlap)


def shrink_of(parts):
    total = (parts[0][...] + parts[1][...]) + (parts[2][...] + parts[3][...])
    grad = 0.0
    for p in range(NX):
        grad = grad + total[3 * p + 2 : 3 * p + 3, :]
    curv = total[3 * NX : 3 * NX + 1, :]
    step = jnp.sum(grad, axis=1, keepdims=True) / (jnp.sum(curv, axis=1, keepdims=True) + EPS)
    norms, level = [], 0.0
    for p in range(NX):
        jj, jc, cc = (total[3 * p + k : 3 * p + k + 1, :] for k in range(3))
        square = jj + 2.0 * step * jc + step * step * cc
        norms.append(jnp.sqrt(jnp.maximum(square, 0.0) + EPS))
        level = level + norms[-1]
    level = jnp.sum(level, axis=1, keepdims=True) / (NX * KZ)
    return step, [jnp.maximum(0.0, 1.0 - SHRINK * level / n) for n in norms]


def second_corr(g0, g1, g2, g3, corr_in, s0, s1, s2, s3, jumps_out, corr_out, stats):
    place = places()
    groups = (g0, g1, g2, g3)
    after = [g[2 * KZ + 3 : 2 * KZ + 4, :] for g in groups]
    overlap = [gram(a)[0] for a in after]
    step, factor = shrink_of((s0, s1, s2, s3))
    jumps, change, sums, weighted = [], [], [], []
    for p in range(NX):
        j = groups[p][0:KZ, :]
        new = factor[p] * (j + step * corr_in[p])
        d = new - j
        jumps_out[p] = new
        jumps.append(new)
        change.append(d)
        sums.append(jnp.sum(d, axis=1, keepdims=True))
        weighted.append(jnp.sum(d * after[p], axis=1, keepdims=True))
    before, behind = carries(place, sums, weighted)
    corr = []
    for p in range(NX):
        c = corr_in[p] - dot(change[p], overlap[p]) - before[p] * after[p] - behind[p]
        corr_out[p] = c
        corr.append(c)
    write_stats(stats, place, jumps, corr, after, overlap)


def finish(bins, signal, g0, jumps_in, corr_in, s0, s1, s2, s3, resid, jumps_out):
    place = places()
    z = lax.axis_index("z")
    width = signal.shape[1]
    step, factor = shrink_of((s0, s1, s2, s3))
    left = jnp.zeros((KZ, KZ), F32)
    for p in range(NX - 1, -1, -1):
        new = factor[p] * (jumps_in[p] + step * corr_in[p])
        if p:
            left += jnp.where(place[p] < place[0], new, 0.0)
    left = jnp.sum(left, axis=1, keepdims=True)
    marks = (bins - 1.0) - g0[2 * KZ + 3 : 2 * KZ + 4, :]
    wide = jnp.broadcast_to(marks, (KZ, KZ)).T
    start = ((place[0] * NZ + z) * width).astype(F32)
    mine = pltpu.roll(new, lax.rem(KZ - z * KD, KZ), 1)
    jumps_out[...] = mine[:, :KD]
    part = pieces(new)
    for k in range(width // KZ):
        bin_at = lax.broadcasted_iota(jnp.int32, (KZ, KZ), 1).astype(F32) + (start + k * KZ)
        mask = (wide < bin_at).astype(BF16)
        fit = jnp.zeros((KZ, KZ), F32)
        for piece in part[::-1]:
            fit += jnp.dot(piece, mask, preferred_element_type=F32)
        here = slice(k * KZ, (k + 1) * KZ)
        resid[:, here] = signal[:, here] - (fit + left)


def over_samples(stats):
    stats = stats + lax.ppermute(stats, "core", [(0, 1), (1, 0)])
    ring = lambda k: [(i, (i + k) % NY) for i in range(NY)]
    return [stats] + [lax.ppermute(stats, "y", ring(k)) for k in range(1, NY)]


def body(signal, jumps, breaks):
    rows, width = signal.shape
    bins = float(width * NX * NZ)
    (mine,) = call(local_sums, [(2 * KD + 8, rows)], 3, smem=1)(breaks, signal, jumps)
    near = lax.all_to_all(jnp.broadcast_to(mine[None], (NZ,) + mine.shape), "z", 0, 0, tiled=False)
    (group,) = call(functools.partial(group_sums, bins), [(2 * KZ + 8, rows)], 1)(near)
    ring = lambda k: [(i, (i + k) % NX) for i in range(NX)]
    groups = [group] + [lax.ppermute(group, "x", ring(k)) for k in (1, 2, 3)]
    corr, stats = call(first_corr, [(NX, rows, KZ), (16, KZ)], 4)(*groups)
    parts = over_samples(stats)
    jumps1, corr, stats = call(second_corr, [(NX, rows, KZ), (NX, rows, KZ), (16, KZ)], 9)(*groups, corr, *parts)
    parts = over_samples(stats)
    resid, jumps2 = call(functools.partial(finish, bins), [(rows, width), (rows, KD)], 8)(signal, group, jumps1, corr, *parts)
    return resid, jumps2


def solution(mesh):
    fine = Mesh(mesh.devices.reshape(NX, NZ, NY, NC), ("x", "z", "y", "core"))
    both = P(("y", "core"), ("x", "z"))
    return jax.shard_map(
        body,
        mesh=fine,
        in_specs=(both, both, P(("x", "z"))),
        out_specs=(both, both),
        check_vma=False,
    )
```

```python
import functools

import jax
import jax.numpy as jnp
from jax import lax
from jax.experimental import pallas as pl
from jax.experimental.pallas import tpu as pltpu
from jax.sharding import Mesh, PartitionSpec as P

EPS = 1e-06
SHRINK = 0.5
NX, NZ, NY, NC = 4, 8, 4, 2
KD = 32
KZ = KD * NZ
F32 = jnp.float32
BF16 = jnp.bfloat16
VMEM = pl.BlockSpec(memory_space=pltpu.VMEM)
SMEM = pl.BlockSpec(memory_space=pltpu.SMEM)
HBM = pl.BlockSpec(memory_space=pltpu.HBM)
CHUNK = 256


def pieces(v):
    hi = v.astype(BF16)
    rest = v - hi.astype(F32)
    mid = rest.astype(BF16)
    low = (rest - mid.astype(F32)).astype(BF16)
    return hi, mid, low


def mul(a, b):
    return jnp.dot(a, b, preferred_element_type=F32)


def times_overlap(v, overlap):
    high, low = overlap
    a, b, _ = pieces(v)
    return (mul(b, high) + mul(a, low)) + mul(a, high)


def call(kernel, out_shape, in_specs, out_specs=None, scratch=()):
    return pl.pallas_call(
        kernel,
        out_shape=[jax.ShapeDtypeStruct(s, F32) for s in out_shape],
        in_specs=in_specs,
        out_specs=out_specs or [VMEM] * len(out_shape),
        scratch_shapes=list(scratch),
        compiler_params=pltpu.CompilerParams(vmem_limit_bytes=32 << 20),
    )


def local_sums(breaks, signal, jumps, out, at_smem, held, sems, sem2):
    rows, width = signal.shape
    marks_in = pltpu.make_async_copy(breaks, at_smem, sem2.at[0])
    marks_in.start()
    parts = [slice(k, k + CHUNK) for k in range(0, width, CHUNK)]
    copies = [pltpu.make_async_copy(signal.at[:, part], held.at[:, part], sems.at[i]) for i, part in enumerate(parts)]
    for copy in copies:
        copy.start()
    jumps_in = pltpu.make_async_copy(jumps, out.at[0:KD, :], sem2.at[1])
    jumps_in.start()
    z = lax.axis_index("z")
    start = (lax.axis_index("x") * NZ + z) * width
    sub = lax.broadcasted_iota(jnp.int32, (40, 128), 0)
    lane = lax.broadcasted_iota(jnp.int32, (8, KZ), 1)
    at = jnp.where(sub == KD, -1, width)
    row = jnp.zeros((8, KZ), jnp.int32)
    marks_in.wait()
    for k in range(KD):
        mark = at_smem[k]
        at = jnp.where(sub == k, mark - start, at)
        row = jnp.where(lane == z * KD + k, mark, row)
    at = jnp.concatenate([at] * (CHUNK // 128), axis=1)
    bin_at = lax.broadcasted_iota(jnp.int32, (40, CHUNK), 1)
    total = jnp.zeros((40, rows), F32)
    for copy, part in zip(copies, parts):
        mask = (bin_at + part.start > at).astype(BF16)
        copy.wait()
        for piece in pieces(held[:, part])[::-1]:
            total += lax.dot_general(mask, piece, (((1,), (1,)), ((), ())), preferred_element_type=F32)
    out[KD : 2 * KD, :] = total[:KD]
    sub8 = lax.broadcasted_iota(jnp.int32, (8, KZ), 0)
    out[2 * KD :, :] = jnp.where(sub8 == 1, row.astype(F32), total[KD:])
    jumps_in.wait()


def gram(after):
    wide = jnp.broadcast_to(after, (KZ, KZ))
    both = jnp.minimum(wide, wide.T)
    high = both.astype(BF16)
    return high, (both - high.astype(F32)).astype(BF16)


def column_sum(v):
    return jnp.sum(v, axis=0, keepdims=True)


TOTAL, JUMPS, WEIGHTED, AFTER, CORR = range(5)


def group_sums(bins, got, big, small):
    head = got[...]
    after = (bins - 1.0) - column_sum(head[:, 2 * KD + 1, :])
    wide = jnp.broadcast_to(after, (KZ, KZ)).T
    overlap = jnp.minimum(jnp.broadcast_to(after, (KZ, KZ)), wide)
    jumps = head[:, :KD, :].reshape(KZ, KZ)
    later = jnp.zeros((1, KZ), F32)
    behind = [None] * NZ
    for z in range(NZ - 1, -1, -1):
        behind[z] = head[z, KD : 2 * KD, :] + later
        later = later + head[z, 2 * KD : 2 * KD + 1, :]
    own = jnp.dot(overlap, jumps, precision=lax.Precision.HIGHEST, preferred_element_type=F32)
    corr = jnp.concatenate(behind, axis=0) - own
    small[TOTAL : TOTAL + 1, :] = later
    small[JUMPS : JUMPS + 1, :] = column_sum(jumps)
    small[WEIGHTED : WEIGHTED + 1, :] = column_sum(jumps * wide)
    small[AFTER : AFTER + 1, :] = after
    small[CORR : CORR + 1, :] = column_sum(corr)
    small[CORR + 1 :, :] = jnp.zeros((7 - CORR, KZ), F32)
    big[0:KZ, :] = jumps.T
    big[KZ:, :] = corr.T


def places():
    x = lax.axis_index("x")
    return [lax.rem(x + NX - k, NX) for k in range(NX)]


def weights(place):
    one = lambda c: jnp.where(c, 1.0, 0.0).astype(F32)
    return [[one(place[q] < place[p]) for q in range(NX)] for p in range(NX)]


def weigh(before, p, values, later=False):
    out = 0.0
    for q in range(NX):
        if q != p:
            out = out + (before[q][p] if later else before[p][q]) * values[q]
    return out


def base_rows(before, smalls):
    row = lambda p, k: smalls[p][k : k + 1, :]
    lower = [weigh(before, p, [row(q, JUMPS) for q in range(NX)]) for p in range(NX)]
    upper = [weigh(before, p, [row(q, TOTAL) - row(q, WEIGHTED) for q in range(NX)], True) for p in range(NX)]
    return lower, upper


def own_stats(big, ms, stats):
    place = places()
    smalls = [ms.at[k] for k in place]
    m0 = smalls[0]
    before = weights(place)
    lower, upper = base_rows(before, smalls)
    after = m0[AFTER : AFTER + 1, :]
    columns = jnp.concatenate([lower[0], upper[0]] + [jnp.zeros((6, KZ), F32)], axis=0).T
    jumps = big[0:KZ, :]
    corr = big[KZ:, :] + columns[:, 1:2] - columns[:, 0:1] * after
    sums = []
    for p in range(NX):
        reach = jnp.sum(smalls[p][AFTER : AFTER + 1, :], axis=1, keepdims=True)
        sums.append(smalls[p][CORR : CORR + 1, :] + float(KZ) * upper[p] - reach * lower[p])
    lead = weigh(before, 0, sums)
    weighted = jnp.sum(corr * after, axis=1, keepdims=True)
    cross = 2.0 * jnp.sum(weighted * jnp.broadcast_to(lead, (8, KZ)).T[:, 0:1])
    curv = column_sum(corr * times_overlap(corr, gram(after)))
    lane = lax.broadcasted_iota(jnp.int32, (1, KZ), 1)
    stats[0:1, :] = column_sum(jumps * jumps)
    stats[1:2, :] = column_sum(jumps * corr)
    stats[2:3, :] = column_sum(corr * corr)
    stats[3:4, :] = curv + jnp.where(lane == 0, cross, 0.0)
    stats[4:, :] = jnp.zeros((4, KZ), F32)


def shrink_of(rows):
    grad, curv = rows(0, 2), rows(0, 3)
    for p in range(1, NX):
        grad, curv = grad + rows(p, 2), curv + rows(p, 3)
    step = jnp.sum(grad, axis=1, keepdims=True) / (jnp.sum(curv, axis=1, keepdims=True) + EPS)
    norms, level = [], 0.0
    for p in range(NX):
        square = rows(p, 0) + 2.0 * step * rows(p, 1) + step * step * rows(p, 2)
        norms.append(jnp.sqrt(jnp.maximum(square, 0.0) + EPS))
        level = level + norms[-1]
    level = jnp.sum(level, axis=1, keepdims=True) / (NX * KZ)
    return step, [jnp.maximum(0.0, 1.0 - SHRINK * level / n) for n in norms]


def second_corr(b0, b1, b2, b3, ms, ss, jumps_out, corr_out, stats):
    place = places()
    smalls = [ms.at[k] for k in place]
    bigs, sums_in = (b0, b1, b2, b3), [ss.at[k] for k in place]
    before = weights(place)
    after = [m[AFTER : AFTER + 1, :] for m in smalls]
    overlap = [gram(a) for a in after]
    lower, upper = base_rows(before, smalls)
    columns = jnp.concatenate(lower + upper, axis=0).T
    step, factor = shrink_of(lambda p, k: sums_in[p][k : k + 1, :])
    jumps, corr, change, sums, weighted = [], [], [], [], []
    for p in range(NX):
        j = bigs[p][0:KZ, :]
        c = bigs[p][KZ:, :] + columns[:, NX + p : NX + p + 1] - columns[:, p : p + 1] * after[p]
        new = factor[p] * (j + step * c)
        d = new - j
        jumps_out[p] = new
        jumps.append(new)
        corr.append(c)
        change.append(d)
        sums.append(jnp.sum(d, axis=1, keepdims=True))
        weighted.append(jnp.sum(d * after[p], axis=1, keepdims=True))
    for p in range(NX):
        low, high = weigh(before, p, sums), weigh(before, p, weighted, True)
        corr[p] = corr[p] - times_overlap(change[p], overlap[p]) - low * after[p] - high
        corr_out[p] = corr[p]
    curv = jnp.zeros((1, KZ), F32)
    for p in range(NX):
        c, j = corr[p], jumps[p]
        sums[p] = jnp.sum(c, axis=1, keepdims=True)
        weighted[p] = jnp.sum(c * after[p], axis=1, keepdims=True)
        stats[4 * p : 4 * p + 1, :] = column_sum(j * j)
        stats[4 * p + 1 : 4 * p + 2, :] = column_sum(j * c)
        stats[4 * p + 2 : 4 * p + 3, :] = column_sum(c * c)
        curv += column_sum(c * times_overlap(c, overlap[p]))
    cross = jnp.zeros((KZ, 1), F32)
    for p in range(NX):
        cross += weighted[p] * weigh(before, p, sums)
    lane = lax.broadcasted_iota(jnp.int32, (1, KZ), 1)
    stats[3:4, :] = curv + jnp.where(lane == 0, 2.0 * jnp.sum(cross), 0.0)
    for p in range(1, NX):
        stats[4 * p + 3 : 4 * p + 4, :] = jnp.zeros((1, KZ), F32)


def finish(bins, signal, m0, jumps_in, corr_in, s0, s1, s2, s3, resid, jumps_out, held, sems):
    before = weights(places())[0]
    x, z = lax.axis_index("x"), lax.axis_index("z")
    width = signal.shape[1]
    total = (s0[...] + s1[...]) + (s2[...] + s3[...])
    step, factor = shrink_of(lambda p, k: total[4 * p + k : 4 * p + k + 1, :])
    left = jnp.zeros((KZ, KZ), F32)
    for p in range(1, NX):
        left += (before[p] * factor[p]) * (jumps_in[p] + step * corr_in[p])
    left = jnp.sum(left, axis=1, keepdims=True)
    new = factor[0] * (jumps_in[0] + step * corr_in[0])
    marks = (bins - 1.0) - m0[AFTER : AFTER + 1, :]
    wide = jnp.broadcast_to(marks, (KZ, KZ)).T
    start = ((x * NZ + z) * width).astype(F32)
    part = pieces(new)
    copies = []
    for i in range(width // CHUNK):
        bin_at = lax.broadcasted_iota(jnp.int32, (KZ, CHUNK), 1).astype(F32) + (start + i * CHUNK)
        mask = (wide < bin_at).astype(BF16)
        fit = jnp.zeros((KZ, CHUNK), F32)
        for piece in part[::-1]:
            fit += mul(piece, mask)
        here = slice(i * CHUNK, (i + 1) * CHUNK)
        held[:, here] = signal[:, here] - (fit + left)
        copies.append(pltpu.make_async_copy(held.at[:, here], resid.at[:, here], sems.at[i]))
        copies[-1].start()
    jumps_out[...] = pltpu.roll(new, lax.rem(KZ - z * KD, KZ), 1)[:, :128].T[:KD]
    for copy in copies:
        copy.wait()


def round_x(block):
    ring = lambda k: [(i, (i + k) % NX) for i in range(NX)]
    return [block] + [lax.ppermute(block, "x", ring(k)) for k in range(1, NX)]


def over_samples(stats):
    stats = stats + lax.ppermute(stats, "core", [(0, 1), (1, 0)])
    ring = lambda k: [(i, (i + k) % NY) for i in range(NY)]
    return [stats] + [lax.ppermute(stats, "y", ring(k)) for k in range(1, NY)]


def body(signal, jumps, breaks):
    rows, width = signal.shape
    bins = float(width * NX * NZ)
    slab = [pltpu.VMEM((rows, width), F32), pltpu.SemaphoreType.DMA((width // CHUNK,))]
    first = call(
        local_sums,
        [(2 * KD + 8, rows)],
        [HBM] * 3,
        scratch=[pltpu.SMEM((KD,), jnp.int32)] + slab + [pltpu.SemaphoreType.DMA((2,))],
    )
    (mine,) = first(*[pltpu.with_memory_space_constraint(a, pltpu.HBM) for a in (breaks, signal, jumps.T)])
    near = lax.all_to_all(jnp.broadcast_to(mine[None], (NZ,) + mine.shape), "z", 0, 0, tiled=False)
    big, small = call(functools.partial(group_sums, bins), [(2 * KZ, rows), (8, rows)], [VMEM])(near)
    ring = lambda k: [(i, (i + k) % NX) for i in range(NX)]
    b1, b3 = lax.ppermute(big, "x", ring(1)), lax.ppermute(big, "x", ring(3))
    smalls = lax.all_to_all(jnp.broadcast_to(small[None], (NX,) + small.shape), "x", 0, 0, tiled=False)
    bg, smalls = lax.optimization_barrier((big, smalls))
    bigs = [big, b1, lax.ppermute(bg, "x", ring(2)), b3]
    (stats,) = call(own_stats, [(8, KZ)], [VMEM] * 2)(big, smalls)
    stats = stats + lax.ppermute(stats, "core", [(0, 1), (1, 0)])
    stats = lax.all_to_all(jnp.broadcast_to(stats[None], (NY,) + stats.shape), "y", 0, 0, tiled=False).sum(0)
    sums = lax.all_to_all(jnp.broadcast_to(stats[None], (NX,) + stats.shape), "x", 0, 0, tiled=False)
    jumps1, corr, stats = call(second_corr, [(NX, rows, KZ), (NX, rows, KZ), (16, KZ)], [VMEM] * 6)(*bigs, smalls, sums)
    parts = over_samples(stats)
    last = call(functools.partial(finish, bins), [(rows, width), (KD, rows)], [VMEM] * 8, [HBM, VMEM], slab)
    resid, jumps2 = last(signal, small, jumps1, corr, *parts)
    return resid, jumps2.T


def solution(mesh):
    fine = Mesh(mesh.devices.reshape(NX, NZ, NY, NC), ("x", "z", "y", "core"))
    both = P(("y", "core"), ("x", "z"))
    return jax.shard_map(
        body,
        mesh=fine,
        in_specs=(both, both, P(("x", "z"))),
        out_specs=(both, both),
        check_vma=False,
    )
```

```python
import functools

import jax
import jax.numpy as jnp
from jax import lax
from jax.experimental import pallas as pl
from jax.experimental.pallas import tpu as pltpu
from jax.sharding import Mesh, PartitionSpec as P

EPS = 1e-06
SHRINK = 0.5
NX, NZ, NY, NC = 4, 8, 4, 2
KD = 32
KZ = KD * NZ
F32 = jnp.float32
BF16 = jnp.bfloat16
VMEM = pl.BlockSpec(memory_space=pltpu.VMEM)
SMEM = pl.BlockSpec(memory_space=pltpu.SMEM)
HBM = pl.BlockSpec(memory_space=pltpu.HBM)
CHUNK = 256
TURN_X = [3, 0, 1, 2]
TURN_Y = [3, 0, 1, 2]
TURN_Z = [6, 7, 0, 1, 2, 3, 4, 5]
HALVES = (slice(0, 128), slice(128, 256))


def pieces(v):
    hi = v.astype(BF16)
    rest = v - hi.astype(F32)
    mid = rest.astype(BF16)
    low = (rest - mid.astype(F32)).astype(BF16)
    return hi, mid, low


def mul(a, b):
    return jnp.dot(a, b, preferred_element_type=F32)


def times_overlap(v, overlap):
    high, low = overlap
    a, b, _ = pieces(v)
    return (mul(b, high) + mul(a, low)) + mul(a, high)


def call(kernel, out_shape, in_specs, out_specs=None, scratch=()):
    return pl.pallas_call(
        kernel,
        out_shape=[jax.ShapeDtypeStruct(s, F32) for s in out_shape],
        in_specs=in_specs,
        out_specs=out_specs or [VMEM] * len(out_shape),
        scratch_shapes=list(scratch),
        compiler_params=pltpu.CompilerParams(vmem_limit_bytes=32 << 20),
    )


def local_sums(breaks, signal, jumps, out, at_smem, held, sems, sem2):
    rows, width = signal.shape
    marks_in = pltpu.make_async_copy(breaks, at_smem, sem2.at[0])
    marks_in.start()
    parts = [slice(k, k + CHUNK) for k in range(0, width, CHUNK)]
    copies = [pltpu.make_async_copy(signal.at[:, part], held.at[:, part], sems.at[i]) for i, part in enumerate(parts)]
    for copy in copies:
        copy.start()
    jumps_in = [pltpu.make_async_copy(jumps.at[:, half], out.at[i * KD : (i + 1) * KD, :], sem2.at[1 + i]) for i, half in enumerate(HALVES)]
    for copy in jumps_in:
        copy.start()
    z = lax.axis_index("z")
    start = (lax.axis_index("x") * NZ + z) * width
    sub = lax.broadcasted_iota(jnp.int32, (40, 128), 0)
    lane = lax.broadcasted_iota(jnp.int32, (8, 128), 1)
    at = jnp.where(sub == KD, -1, width)
    row = jnp.zeros((8, 128), jnp.int32)
    shift = lax.rem(z * KD, 128)
    marks_in.wait()
    for k in range(KD):
        mark = at_smem[k]
        at = jnp.where(sub == k, mark - start, at)
        row = jnp.where(lane == shift + k, mark, row)
    at = jnp.concatenate([at] * (CHUNK // 128), axis=1)
    bin_at = lax.broadcasted_iota(jnp.int32, (40, CHUNK), 1)
    total = jnp.zeros((40, rows), F32)
    for copy, part in zip(copies, parts):
        mask = (bin_at + part.start > at).astype(BF16)
        copy.wait()
        for piece in pieces(held[:, part])[::-1]:
            total += lax.dot_general(mask, piece, (((1,), (1,)), ((), ())), preferred_element_type=F32)
    tail = row.astype(F32)
    sub8 = lax.broadcasted_iota(jnp.int32, (8, 128), 0)
    for i, half in enumerate(HALVES):
        out[(2 + i) * KD : (3 + i) * KD, :] = total[:KD, half]
        tail = jnp.where(sub8 == i, total[KD : KD + 1, half], tail)
    out[4 * KD :, :] = tail
    for copy in jumps_in:
        copy.wait()


def gram(after):
    wide = jnp.broadcast_to(after, (KZ, KZ))
    both = jnp.minimum(wide, wide.T)
    high = both.astype(BF16)
    return high, (both - high.astype(F32)).astype(BF16)


def column_sum(v):
    return jnp.sum(v, axis=0, keepdims=True)


TOTAL, JUMPS, WEIGHTED, AFTER, CORR = range(5)


def group_sums(bins, got, big, small):
    at = [TURN_Z.index(z) for z in range(NZ)]
    marks = [sum(got[at[z], 4 * KD + 2 : 4 * KD + 3, :] for z in range(i * 4, i * 4 + 4)) for i in range(2)]
    after = (bins - 1.0) - jnp.concatenate(marks, axis=1)
    wide = jnp.broadcast_to(after, (KZ, KZ)).T
    overlap = jnp.minimum(jnp.broadcast_to(after, (KZ, KZ)), wide)
    jumps = [jnp.concatenate([got[k, i * KD : (i + 1) * KD, :] for k in at], axis=0) for i in range(2)]
    jumps = jnp.concatenate(jumps, axis=1)
    later, behind = [], []
    for i in range(2):
        total = jnp.zeros((1, 128), F32)
        part = [None] * NZ
        for z in range(NZ - 1, -1, -1):
            part[z] = got[at[z], (2 + i) * KD : (3 + i) * KD, :] + total
            total = total + got[at[z], 4 * KD + i : 4 * KD + i + 1, :]
        later.append(total)
        behind.append(jnp.concatenate(part, axis=0))
    later = jnp.concatenate(later, axis=1)
    own = jnp.dot(overlap, jumps, precision=lax.Precision.HIGHEST, preferred_element_type=F32)
    corr = jnp.concatenate(behind, axis=1) - own
    small[TOTAL : TOTAL + 1, :] = later
    small[JUMPS : JUMPS + 1, :] = column_sum(jumps)
    small[WEIGHTED : WEIGHTED + 1, :] = column_sum(jumps * wide)
    small[AFTER : AFTER + 1, :] = after
    small[CORR : CORR + 1, :] = column_sum(corr)
    small[CORR + 1 :, :] = jnp.zeros((7 - CORR, KZ), F32)
    big[0:KZ, :] = jumps.T
    big[KZ:, :] = corr.T


def places():
    x = lax.axis_index("x")
    return [lax.rem(x + NX - k, NX) for k in range(NX)]


def turn_x(k):
    return lax.rem(k + 1, NX)


def weights(place):
    one = lambda c: jnp.where(c, 1.0, 0.0).astype(F32)
    return [[one(place[q] < place[p]) for q in range(NX)] for p in range(NX)]


def weigh(before, p, values, later=False):
    out = 0.0
    for q in range(NX):
        if q != p:
            out = out + (before[q][p] if later else before[p][q]) * values[q]
    return out


def base_rows(before, smalls):
    row = lambda p, k: smalls[p][k : k + 1, :]
    lower = [weigh(before, p, [row(q, JUMPS) for q in range(NX)]) for p in range(NX)]
    upper = [weigh(before, p, [row(q, TOTAL) - row(q, WEIGHTED) for q in range(NX)], True) for p in range(NX)]
    return lower, upper


def own_stats(big, ms, stats):
    place = places()
    smalls = [ms.at[turn_x(k)] for k in place]
    m0 = smalls[0]
    before = weights(place)
    lower, upper = base_rows(before, smalls)
    after = m0[AFTER : AFTER + 1, :]
    columns = jnp.concatenate([lower[0], upper[0]] + [jnp.zeros((6, KZ), F32)], axis=0).T
    jumps = big[0:KZ, :]
    corr = big[KZ:, :] + columns[:, 1:2] - columns[:, 0:1] * after
    sums = []
    for p in range(NX):
        reach = jnp.sum(smalls[p][AFTER : AFTER + 1, :], axis=1, keepdims=True)
        sums.append(smalls[p][CORR : CORR + 1, :] + float(KZ) * upper[p] - reach * lower[p])
    lead = weigh(before, 0, sums)
    weighted = jnp.sum(corr * after, axis=1, keepdims=True)
    cross = 2.0 * jnp.sum(weighted * jnp.broadcast_to(lead, (8, KZ)).T[:, 0:1])
    curv = column_sum(corr * times_overlap(corr, gram(after)))
    lane = lax.broadcasted_iota(jnp.int32, (1, KZ), 1)
    stats[0:1, :] = column_sum(jumps * jumps)
    stats[1:2, :] = column_sum(jumps * corr)
    stats[2:3, :] = column_sum(corr * corr)
    stats[3:4, :] = curv + jnp.where(lane == 0, cross, 0.0)
    stats[4:, :] = jnp.zeros((4, KZ), F32)


def shrink_of(rows):
    grad, curv = rows(0, 2), rows(0, 3)
    for p in range(1, NX):
        grad, curv = grad + rows(p, 2), curv + rows(p, 3)
    step = jnp.sum(grad, axis=1, keepdims=True) / (jnp.sum(curv, axis=1, keepdims=True) + EPS)
    norms, level = [], 0.0
    for p in range(NX):
        square = rows(p, 0) + 2.0 * step * rows(p, 1) + step * step * rows(p, 2)
        norms.append(jnp.sqrt(jnp.maximum(square, 0.0) + EPS))
        level = level + norms[-1]
    level = jnp.sum(level, axis=1, keepdims=True) / (NX * KZ)
    return step, [jnp.maximum(0.0, 1.0 - SHRINK * level / n) for n in norms]


def second_corr(b0, b1, b2, b3, ms, ss, jumps_out, corr_out, stats):
    place = places()
    smalls = [ms.at[turn_x(k)] for k in place]
    bigs, sums_in = (b0, b1, b2, b3), [ss.at[turn_x(k)] for k in place]
    before = weights(place)
    after = [m[AFTER : AFTER + 1, :] for m in smalls]
    overlap = [gram(a) for a in after]
    lower, upper = base_rows(before, smalls)
    columns = jnp.concatenate(lower + upper, axis=0).T
    step, factor = shrink_of(lambda p, k: sums_in[p][k : k + 1, :])
    jumps, corr, change, sums, weighted = [], [], [], [], []
    for p in range(NX):
        j = bigs[p][0:KZ, :]
        c = bigs[p][KZ:, :] + columns[:, NX + p : NX + p + 1] - columns[:, p : p + 1] * after[p]
        new = factor[p] * (j + step * c)
        d = new - j
        jumps_out[p] = new
        jumps.append(new)
        corr.append(c)
        change.append(d)
        sums.append(jnp.sum(d, axis=1, keepdims=True))
        weighted.append(jnp.sum(d * after[p], axis=1, keepdims=True))
    for p in range(NX):
        low, high = weigh(before, p, sums), weigh(before, p, weighted, True)
        corr[p] = corr[p] - times_overlap(change[p], overlap[p]) - low * after[p] - high
        corr_out[p] = corr[p]
    curv = jnp.zeros((1, KZ), F32)
    for p in range(NX):
        c, j = corr[p], jumps[p]
        sums[p] = jnp.sum(c, axis=1, keepdims=True)
        weighted[p] = jnp.sum(c * after[p], axis=1, keepdims=True)
        stats[4 * p : 4 * p + 1, :] = column_sum(j * j)
        stats[4 * p + 1 : 4 * p + 2, :] = column_sum(j * c)
        stats[4 * p + 2 : 4 * p + 3, :] = column_sum(c * c)
        curv += column_sum(c * times_overlap(c, overlap[p]))
    cross = jnp.zeros((KZ, 1), F32)
    for p in range(NX):
        cross += weighted[p] * weigh(before, p, sums)
    lane = lax.broadcasted_iota(jnp.int32, (1, KZ), 1)
    stats[3:4, :] = curv + jnp.where(lane == 0, 2.0 * jnp.sum(cross), 0.0)
    for p in range(1, NX):
        stats[4 * p + 3 : 4 * p + 4, :] = jnp.zeros((1, KZ), F32)


def finish(bins, signal, m0, jumps_in, corr_in, s0, s1, s2, s3, resid, jumps_out, held, sems):
    before = weights(places())[0]
    x, z = lax.axis_index("x"), lax.axis_index("z")
    width = signal.shape[1]
    total = (s0[...] + s1[...]) + (s2[...] + s3[...])
    step, factor = shrink_of(lambda p, k: total[4 * p + k : 4 * p + k + 1, :])
    left = jnp.zeros((KZ, KZ), F32)
    for p in range(1, NX):
        left += (before[p] * factor[p]) * (jumps_in[p] + step * corr_in[p])
    left = jnp.sum(left, axis=1, keepdims=True)
    new = factor[0] * (jumps_in[0] + step * corr_in[0])
    marks = (bins - 1.0) - m0[AFTER : AFTER + 1, :]
    wide = jnp.broadcast_to(marks, (KZ, KZ)).T
    start = ((x * NZ + z) * width).astype(F32)
    part = pieces(new)
    copies = []
    for i in range(width // CHUNK):
        bin_at = lax.broadcasted_iota(jnp.int32, (KZ, CHUNK), 1).astype(F32) + (start + i * CHUNK)
        mask = (wide < bin_at).astype(BF16)
        fit = jnp.zeros((KZ, CHUNK), F32)
        for piece in part[::-1]:
            fit += mul(piece, mask)
        here = slice(i * CHUNK, (i + 1) * CHUNK)
        held[:, here] = signal[:, here] - (fit + left)
        copies.append(pltpu.make_async_copy(held.at[:, here], resid.at[:, here], sems.at[i]))
        copies[-1].start()
    jumps_out[...] = pltpu.roll(new, lax.rem(KZ - z * KD, KZ), 1)[:, :128].T[:KD]
    for copy in copies:
        copy.wait()


def round_x(block):
    ring = lambda k: [(i, (i + k) % NX) for i in range(NX)]
    return [block] + [lax.ppermute(block, "x", ring(k)) for k in range(1, NX)]


def over_samples(stats):
    stats = stats + lax.ppermute(stats, "core", [(0, 1), (1, 0)])
    ring = lambda k: [(i, (i + k) % NY) for i in range(NY)]
    return [stats] + [lax.ppermute(stats, "y", ring(k)) for k in range(1, NY)]


def body(signal, jumps, breaks):
    rows, width = signal.shape
    bins = float(width * NX * NZ)
    slab = [pltpu.VMEM((rows, width), F32), pltpu.SemaphoreType.DMA((width // CHUNK,))]
    first = call(
        local_sums,
        [(4 * KD + 8, rows // 2)],
        [HBM] * 3,
        scratch=[pltpu.SMEM((KD,), jnp.int32)] + slab + [pltpu.SemaphoreType.DMA((3,))],
    )
    (mine,) = first(*[pltpu.with_memory_space_constraint(a, pltpu.HBM) for a in (breaks, signal, jumps.T)])
    near = lax.all_to_all(
        jnp.broadcast_to(mine[None], (NZ,) + mine.shape), "z", 0, 0, axis_index_groups=[TURN_Z], tiled=False
    )
    big, small = call(functools.partial(group_sums, bins), [(2 * KZ, rows), (8, rows)], [VMEM])(near)
    ring = lambda k: [(i, (i + k) % NX) for i in range(NX)]
    b1, b3 = lax.ppermute(big, "x", ring(1)), lax.ppermute(big, "x", ring(3))
    smalls = lax.all_to_all(
        jnp.broadcast_to(small[None], (NX,) + small.shape), "x", 0, 0, axis_index_groups=[TURN_X], tiled=False
    )
    bg, smalls = lax.optimization_barrier((big, smalls))
    bigs = [big, b1, lax.ppermute(bg, "x", ring(2)), b3]
    (stats,) = call(own_stats, [(8, KZ)], [VMEM] * 2)(big, smalls)
    stats = stats + lax.ppermute(stats, "core", [(0, 1), (1, 0)])
    stats = lax.all_to_all(jnp.broadcast_to(stats[None], (NY,) + stats.shape), "y", 0, 0, axis_index_groups=[TURN_Y], tiled=False).sum(0)
    sums = lax.all_to_all(
        jnp.broadcast_to(stats[None], (NX,) + stats.shape), "x", 0, 0, axis_index_groups=[TURN_X], tiled=False
    )
    jumps1, corr, stats = call(second_corr, [(NX, rows, KZ), (NX, rows, KZ), (16, KZ)], [VMEM] * 6)(*bigs, smalls, sums)
    parts = over_samples(stats)
    last = call(functools.partial(finish, bins), [(rows, width), (KD, rows)], [VMEM] * 8, [HBM, VMEM], slab)
    resid, jumps2 = last(signal, small, jumps1, corr, *parts)
    return resid, jumps2.T


def solution(mesh):
    fine = Mesh(mesh.devices.reshape(NX, NZ, NY, NC), ("x", "z", "y", "core"))
    both = P(("y", "core"), ("x", "z"))
    return jax.shard_map(
        body,
        mesh=fine,
        in_specs=(both, both, P(("x", "z"))),
        out_specs=(both, both),
        check_vma=False,
    )
```

```python
import functools

import jax
import jax.numpy as jnp
from jax import lax
from jax.experimental import pallas as pl
from jax.experimental.pallas import tpu as pltpu
from jax.sharding import Mesh, PartitionSpec as P

EPS = 1e-06
SHRINK = 0.5
NX, NZ, NY, NC = 4, 8, 4, 2
KD = 32
KZ = KD * NZ
F32 = jnp.float32
BF16 = jnp.bfloat16
VMEM = pl.BlockSpec(memory_space=pltpu.VMEM)
SMEM = pl.BlockSpec(memory_space=pltpu.SMEM)
HBM = pl.BlockSpec(memory_space=pltpu.HBM)
CHUNK = 256
TURN_X = [3, 0, 1, 2]
TURN_Y = [2, 3, 0, 1]
TURN_Z = [6, 7, 0, 1, 2, 3, 4, 5]
HALVES = (slice(0, 128), slice(128, 256))


def pieces(v):
    hi = v.astype(BF16)
    rest = v - hi.astype(F32)
    mid = rest.astype(BF16)
    low = (rest - mid.astype(F32)).astype(BF16)
    return hi, mid, low


def mul(a, b):
    return jnp.dot(a, b, preferred_element_type=F32)


def times_overlap(v, overlap):
    high, low = overlap
    a, b, _ = pieces(v)
    return (mul(b, high) + mul(a, low)) + mul(a, high)


def call(kernel, out_shape, in_specs, out_specs=None, scratch=()):
    return pl.pallas_call(
        kernel,
        out_shape=[jax.ShapeDtypeStruct(s, F32) for s in out_shape],
        in_specs=in_specs,
        out_specs=out_specs or [VMEM] * len(out_shape),
        scratch_shapes=list(scratch),
        compiler_params=pltpu.CompilerParams(vmem_limit_bytes=32 << 20),
    )


def local_sums(breaks, signal, jumps, out, at_smem, held, sems, sem2):
    rows, width = signal.shape
    marks_in = pltpu.make_async_copy(breaks, at_smem, sem2.at[0])
    marks_in.start()
    parts = [slice(k, k + CHUNK) for k in range(0, width, CHUNK)]
    copies = [pltpu.make_async_copy(signal.at[:, part], held.at[:, part], sems.at[i]) for i, part in enumerate(parts)]
    for copy in copies:
        copy.start()
    jumps_in = [pltpu.make_async_copy(jumps.at[:, half], out.at[i * KD : (i + 1) * KD, :], sem2.at[1 + i]) for i, half in enumerate(HALVES)]
    for copy in jumps_in:
        copy.start()
    z = lax.axis_index("z")
    start = (lax.axis_index("x") * NZ + z) * width
    sub = lax.broadcasted_iota(jnp.int32, (40, 128), 0)
    lane = lax.broadcasted_iota(jnp.int32, (8, 128), 1)
    at = jnp.where(sub == KD, -1, width)
    row = jnp.zeros((8, 128), jnp.int32)
    shift = lax.rem(z * KD, 128)
    marks_in.wait()
    for k in range(KD):
        mark = at_smem[k]
        at = jnp.where(sub == k, mark - start, at)
        row = jnp.where(lane == shift + k, mark, row)
    at = jnp.concatenate([at] * (CHUNK // 128), axis=1)
    bin_at = lax.broadcasted_iota(jnp.int32, (40, CHUNK), 1)
    total = jnp.zeros((40, rows), F32)
    for copy, part in zip(copies, parts):
        mask = (bin_at + part.start > at).astype(BF16)
        copy.wait()
        for piece in pieces(held[:, part])[::-1]:
            total += lax.dot_general(mask, piece, (((1,), (1,)), ((), ())), preferred_element_type=F32)
    tail = row.astype(F32)
    sub8 = lax.broadcasted_iota(jnp.int32, (8, 128), 0)
    for i, half in enumerate(HALVES):
        out[(2 + i) * KD : (3 + i) * KD, :] = total[:KD, half]
        tail = jnp.where(sub8 == i, total[KD : KD + 1, half], tail)
    out[4 * KD :, :] = tail
    for copy in jumps_in:
        copy.wait()


def gram(after):
    wide = jnp.broadcast_to(after, (KZ, KZ))
    both = jnp.minimum(wide, wide.T)
    high = both.astype(BF16)
    return high, (both - high.astype(F32)).astype(BF16)


def column_sum(v):
    return jnp.sum(v, axis=0, keepdims=True)


TOTAL, JUMPS, WEIGHTED, AFTER, CORR = range(5)


def group_sums(bins, got, big, small):
    at = [TURN_Z.index(z) for z in range(NZ)]
    marks = [sum(got[at[z], 4 * KD + 2 : 4 * KD + 3, :] for z in range(i * 4, i * 4 + 4)) for i in range(2)]
    after = (bins - 1.0) - jnp.concatenate(marks, axis=1)
    wide = jnp.broadcast_to(after, (KZ, KZ)).T
    overlap = jnp.minimum(jnp.broadcast_to(after, (KZ, KZ)), wide)
    jumps = [jnp.concatenate([got[k, i * KD : (i + 1) * KD, :] for k in at], axis=0) for i in range(2)]
    jumps = jnp.concatenate(jumps, axis=1)
    later, behind = [], []
    for i in range(2):
        total = jnp.zeros((1, 128), F32)
        part = [None] * NZ
        for z in range(NZ - 1, -1, -1):
            part[z] = got[at[z], (2 + i) * KD : (3 + i) * KD, :] + total
            total = total + got[at[z], 4 * KD + i : 4 * KD + i + 1, :]
        later.append(total)
        behind.append(jnp.concatenate(part, axis=0))
    later = jnp.concatenate(later, axis=1)
    own = jnp.dot(overlap, jumps, precision=lax.Precision.HIGHEST, preferred_element_type=F32)
    corr = jnp.concatenate(behind, axis=1) - own
    small[TOTAL : TOTAL + 1, :] = later
    small[JUMPS : JUMPS + 1, :] = column_sum(jumps)
    small[WEIGHTED : WEIGHTED + 1, :] = column_sum(jumps * wide)
    small[AFTER : AFTER + 1, :] = after
    small[CORR : CORR + 1, :] = column_sum(corr)
    small[CORR + 1 :, :] = jnp.zeros((7 - CORR, KZ), F32)
    big[0:KZ, :] = jumps.T
    big[KZ:, :] = corr.T


def places():
    x = lax.axis_index("x")
    return [lax.rem(x + NX - k, NX) for k in range(NX)]


def turn_x(k):
    return lax.rem(k + 1, NX)


def weights(place):
    one = lambda c: jnp.where(c, 1.0, 0.0).astype(F32)
    return [[one(place[q] < place[p]) for q in range(NX)] for p in range(NX)]


def weigh(before, p, values, later=False):
    out = 0.0
    for q in range(NX):
        if q != p:
            out = out + (before[q][p] if later else before[p][q]) * values[q]
    return out


def base_rows(before, smalls):
    row = lambda p, k: smalls[p][k : k + 1, :]
    lower = [weigh(before, p, [row(q, JUMPS) for q in range(NX)]) for p in range(NX)]
    upper = [weigh(before, p, [row(q, TOTAL) - row(q, WEIGHTED) for q in range(NX)], True) for p in range(NX)]
    return lower, upper


def own_stats(big, ms, stats):
    place = places()
    smalls = [ms.at[turn_x(k)] for k in place]
    m0 = smalls[0]
    before = weights(place)
    lower, upper = base_rows(before, smalls)
    after = m0[AFTER : AFTER + 1, :]
    columns = jnp.concatenate([lower[0], upper[0]] + [jnp.zeros((6, KZ), F32)], axis=0).T
    jumps = big[0:KZ, :]
    corr = big[KZ:, :] + columns[:, 1:2] - columns[:, 0:1] * after
    sums = []
    for p in range(NX):
        reach = jnp.sum(smalls[p][AFTER : AFTER + 1, :], axis=1, keepdims=True)
        sums.append(smalls[p][CORR : CORR + 1, :] + float(KZ) * upper[p] - reach * lower[p])
    lead = weigh(before, 0, sums)
    weighted = jnp.sum(corr * after, axis=1, keepdims=True)
    cross = 2.0 * jnp.sum(weighted * jnp.broadcast_to(lead, (8, KZ)).T[:, 0:1])
    curv = column_sum(corr * times_overlap(corr, gram(after)))
    lane = lax.broadcasted_iota(jnp.int32, (1, KZ), 1)
    stats[0:1, :] = column_sum(jumps * jumps)
    stats[1:2, :] = column_sum(jumps * corr)
    stats[2:3, :] = column_sum(corr * corr)
    stats[3:4, :] = curv + jnp.where(lane == 0, cross, 0.0)
    stats[4:, :] = jnp.zeros((4, KZ), F32)


def shrink_of(rows):
    grad, curv = rows(0, 2), rows(0, 3)
    for p in range(1, NX):
        grad, curv = grad + rows(p, 2), curv + rows(p, 3)
    step = jnp.sum(grad, axis=1, keepdims=True) / (jnp.sum(curv, axis=1, keepdims=True) + EPS)
    norms, level = [], 0.0
    for p in range(NX):
        square = rows(p, 0) + 2.0 * step * rows(p, 1) + step * step * rows(p, 2)
        norms.append(jnp.sqrt(jnp.maximum(square, 0.0) + EPS))
        level = level + norms[-1]
    level = jnp.sum(level, axis=1, keepdims=True) / (NX * KZ)
    return step, [jnp.maximum(0.0, 1.0 - SHRINK * level / n) for n in norms]


def second_corr(b0, b1, b2, b3, ms, ss, jumps_out, corr_out, stats):
    place = places()
    smalls = [ms.at[turn_x(k)] for k in place]
    bigs, sums_in = (b0, b1, b2, b3), [ss.at[turn_x(k)] for k in place]
    before = weights(place)
    after = [m[AFTER : AFTER + 1, :] for m in smalls]
    overlap = [gram(a) for a in after]
    lower, upper = base_rows(before, smalls)
    columns = jnp.concatenate(lower + upper, axis=0).T
    step, factor = shrink_of(lambda p, k: sums_in[p][k : k + 1, :])
    jumps, corr, change, sums, weighted = [], [], [], [], []
    for p in range(NX):
        j = bigs[p][0:KZ, :]
        c = bigs[p][KZ:, :] + columns[:, NX + p : NX + p + 1] - columns[:, p : p + 1] * after[p]
        new = factor[p] * (j + step * c)
        d = new - j
        jumps_out[p] = new
        jumps.append(new)
        corr.append(c)
        change.append(d)
        sums.append(jnp.sum(d, axis=1, keepdims=True))
        weighted.append(jnp.sum(d * after[p], axis=1, keepdims=True))
    for p in range(NX):
        low, high = weigh(before, p, sums), weigh(before, p, weighted, True)
        corr[p] = corr[p] - times_overlap(change[p], overlap[p]) - low * after[p] - high
        corr_out[p] = corr[p]
    curv = jnp.zeros((1, KZ), F32)
    for p in range(NX):
        c, j = corr[p], jumps[p]
        sums[p] = jnp.sum(c, axis=1, keepdims=True)
        weighted[p] = jnp.sum(c * after[p], axis=1, keepdims=True)
        stats[4 * p : 4 * p + 1, :] = column_sum(j * j)
        stats[4 * p + 1 : 4 * p + 2, :] = column_sum(j * c)
        stats[4 * p + 2 : 4 * p + 3, :] = column_sum(c * c)
        curv += column_sum(c * times_overlap(c, overlap[p]))
    cross = jnp.zeros((KZ, 1), F32)
    for p in range(NX):
        cross += weighted[p] * weigh(before, p, sums)
    lane = lax.broadcasted_iota(jnp.int32, (1, KZ), 1)
    stats[3:4, :] = curv + jnp.where(lane == 0, 2.0 * jnp.sum(cross), 0.0)
    for p in range(1, NX):
        stats[4 * p + 3 : 4 * p + 4, :] = jnp.zeros((1, KZ), F32)


def finish(bins, signal, m0, jumps_in, corr_in, s0, s1, s2, s3, resid, jumps_out, held, sems):
    before = weights(places())[0]
    x, z = lax.axis_index("x"), lax.axis_index("z")
    width = signal.shape[1]
    total = (s0[...] + s1[...]) + (s2[...] + s3[...])
    step, factor = shrink_of(lambda p, k: total[4 * p + k : 4 * p + k + 1, :])
    left = jnp.zeros((KZ, KZ), F32)
    for p in range(1, NX):
        left += (before[p] * factor[p]) * (jumps_in[p] + step * corr_in[p])
    left = jnp.sum(left, axis=1, keepdims=True)
    new = factor[0] * (jumps_in[0] + step * corr_in[0])
    marks = (bins - 1.0) - m0[AFTER : AFTER + 1, :]
    wide = jnp.broadcast_to(marks, (KZ, KZ)).T
    start = ((x * NZ + z) * width).astype(F32)
    part = pieces(new)
    copies = []
    for i in range(width // CHUNK):
        bin_at = lax.broadcasted_iota(jnp.int32, (KZ, CHUNK), 1).astype(F32) + (start + i * CHUNK)
        mask = (wide < bin_at).astype(BF16)
        fit = jnp.zeros((KZ, CHUNK), F32)
        for piece in part[::-1]:
            fit += mul(piece, mask)
        here = slice(i * CHUNK, (i + 1) * CHUNK)
        held[:, here] = signal[:, here] - (fit + left)
        copies.append(pltpu.make_async_copy(held.at[:, here], resid.at[:, here], sems.at[i]))
        copies[-1].start()
    jumps_out[...] = pltpu.roll(new, lax.rem(KZ - z * KD, KZ), 1)[:, :128].T[:KD]
    for copy in copies:
        copy.wait()


def round_x(block):
    ring = lambda k: [(i, (i + k) % NX) for i in range(NX)]
    return [block] + [lax.ppermute(block, "x", ring(k)) for k in range(1, NX)]


def over_samples(stats):
    stats = stats + lax.ppermute(stats, "core", [(0, 1), (1, 0)])
    return [stats] + [lax.ppermute(stats, "y", [(i, i ^ k) for i in range(NY)]) for k in (1, 2, 3)]


def body(signal, jumps, breaks):
    rows, width = signal.shape
    bins = float(width * NX * NZ)
    slab = [pltpu.VMEM((rows, width), F32), pltpu.SemaphoreType.DMA((width // CHUNK,))]
    first = call(
        local_sums,
        [(4 * KD + 8, rows // 2)],
        [HBM] * 3,
        scratch=[pltpu.SMEM((KD,), jnp.int32)] + slab + [pltpu.SemaphoreType.DMA((3,))],
    )
    (mine,) = first(*[pltpu.with_memory_space_constraint(a, pltpu.HBM) for a in (breaks, signal, jumps.T)])
    near = lax.all_to_all(
        jnp.broadcast_to(mine[None], (NZ,) + mine.shape), "z", 0, 0, axis_index_groups=[TURN_Z], tiled=False
    )
    big, small = call(functools.partial(group_sums, bins), [(2 * KZ, rows), (8, rows)], [VMEM])(near)
    ring = lambda k: [(i, (i + k) % NX) for i in range(NX)]
    b1, b3 = lax.ppermute(big, "x", ring(1)), lax.ppermute(big, "x", ring(3))
    smalls = lax.all_to_all(
        jnp.broadcast_to(small[None], (NX,) + small.shape), "x", 0, 0, axis_index_groups=[TURN_X], tiled=False
    )
    bg, smalls = lax.optimization_barrier((big, smalls))
    bigs = [big, b1, lax.ppermute(bg, "x", ring(2)), b3]
    (stats,) = call(own_stats, [(8, KZ)], [VMEM] * 2)(big, smalls)
    stats = stats + lax.ppermute(stats, "core", [(0, 1), (1, 0)])
    stats = lax.all_to_all(jnp.broadcast_to(stats[None], (NY,) + stats.shape), "y", 0, 0, axis_index_groups=[TURN_Y], tiled=False).sum(0)
    sums = lax.all_to_all(
        jnp.broadcast_to(stats[None], (NX,) + stats.shape), "x", 0, 0, axis_index_groups=[TURN_X], tiled=False
    )
    jumps1, corr, stats = call(second_corr, [(NX, rows, KZ), (NX, rows, KZ), (16, KZ)], [VMEM] * 6)(*bigs, smalls, sums)
    parts = over_samples(stats)
    last = call(functools.partial(finish, bins), [(rows, width), (KD, rows)], [VMEM] * 8, [HBM, VMEM], slab)
    resid, jumps2 = last(signal, small, jumps1, corr, *parts)
    return resid, jumps2.T


def solution(mesh):
    fine = Mesh(mesh.devices.reshape(NX, NZ, NY, NC), ("x", "z", "y", "core"))
    both = P(("y", "core"), ("x", "z"))
    return jax.shard_map(
        body,
        mesh=fine,
        in_specs=(both, both, P(("x", "z"))),
        out_specs=(both, both),
        check_vma=False,
    )
```

```python
import functools

import jax
import jax.numpy as jnp
from jax import lax
from jax.experimental import pallas as pl
from jax.experimental.pallas import tpu as pltpu
from jax.sharding import Mesh, PartitionSpec as P

EPS = 1e-06
SHRINK = 0.5
NX, NZ, NY, NC = 4, 8, 4, 2
KD = 32
KZ = KD * NZ
F32 = jnp.float32
BF16 = jnp.bfloat16
VMEM = pl.BlockSpec(memory_space=pltpu.VMEM)
SMEM = pl.BlockSpec(memory_space=pltpu.SMEM)
HBM = pl.BlockSpec(memory_space=pltpu.HBM)
CHUNK = 256
TURN_X = [3, 0, 1, 2]
TURN_Y = [2, 3, 0, 1]
TURN_Z = [6, 7, 0, 1, 2, 3, 4, 5]
HALVES = (slice(0, 128), slice(128, 256))


def pieces(v):
    hi = v.astype(BF16)
    rest = v - hi.astype(F32)
    mid = rest.astype(BF16)
    low = (rest - mid.astype(F32)).astype(BF16)
    return hi, mid, low


def mul(a, b):
    return jnp.dot(a, b, preferred_element_type=F32)


def times_overlap(v, overlap):
    high, low = overlap
    a, b, _ = pieces(v)
    return (mul(b, high) + mul(a, low)) + mul(a, high)


def call(kernel, out_shape, in_specs, out_specs=None, scratch=()):
    return pl.pallas_call(
        kernel,
        out_shape=[jax.ShapeDtypeStruct(s, F32) for s in out_shape],
        in_specs=in_specs,
        out_specs=out_specs or [VMEM] * len(out_shape),
        scratch_shapes=list(scratch),
        compiler_params=pltpu.CompilerParams(vmem_limit_bytes=32 << 20),
    )


def local_sums(breaks, signal, jumps, out, at_smem, held, sems, sem2):
    rows, width = signal.shape
    marks_in = pltpu.make_async_copy(breaks, at_smem, sem2.at[0])
    marks_in.start()
    parts = [slice(k, k + CHUNK) for k in range(0, width, CHUNK)]
    copies = [pltpu.make_async_copy(signal.at[:, part], held.at[:, part], sems.at[i]) for i, part in enumerate(parts)]
    for copy in copies:
        copy.start()
    jumps_in = [pltpu.make_async_copy(jumps.at[:, half], out.at[i * KD : (i + 1) * KD, :], sem2.at[1 + i]) for i, half in enumerate(HALVES)]
    for copy in jumps_in:
        copy.start()
    z = lax.axis_index("z")
    start = (lax.axis_index("x") * NZ + z) * width
    sub = lax.broadcasted_iota(jnp.int32, (40, 128), 0)
    lane = lax.broadcasted_iota(jnp.int32, (8, 128), 1)
    at = jnp.where(sub == KD, -1, width)
    row = jnp.zeros((8, 128), jnp.int32)
    shift = lax.rem(z * KD, 128)
    marks_in.wait()
    for k in range(KD):
        mark = at_smem[k]
        at = jnp.where(sub == k, mark - start, at)
        row = jnp.where(lane == shift + k, mark, row)
    at = jnp.concatenate([at] * (CHUNK // 128), axis=1)
    bin_at = lax.broadcasted_iota(jnp.int32, (40, CHUNK), 1)
    total = jnp.zeros((40, rows), F32)
    for copy, part in zip(copies, parts):
        mask = (bin_at + part.start > at).astype(BF16)
        copy.wait()
        for piece in pieces(held[:, part])[::-1]:
            total += lax.dot_general(mask, piece, (((1,), (1,)), ((), ())), preferred_element_type=F32)
    tail = row.astype(F32)
    sub8 = lax.broadcasted_iota(jnp.int32, (8, 128), 0)
    for i, half in enumerate(HALVES):
        out[(2 + i) * KD : (3 + i) * KD, :] = total[:KD, half]
        tail = jnp.where(sub8 == i, total[KD : KD + 1, half], tail)
    out[4 * KD :, :] = tail
    for copy in jumps_in:
        copy.wait()


def gram(after):
    wide = jnp.broadcast_to(after, (KZ, KZ))
    both = jnp.minimum(wide, wide.T)
    high = both.astype(BF16)
    return high, (both - high.astype(F32)).astype(BF16)


def column_sum(v):
    return jnp.sum(v, axis=0, keepdims=True)


TOTAL, JUMPS, WEIGHTED, AFTER, CORR = range(5)


def group_sums(bins, got, big, small):
    at = [TURN_Z.index(z) for z in range(NZ)]
    marks = [sum(got[at[z], 4 * KD + 2 : 4 * KD + 3, :] for z in range(i * 4, i * 4 + 4)) for i in range(2)]
    after = (bins - 1.0) - jnp.concatenate(marks, axis=1)
    wide = jnp.broadcast_to(after, (KZ, KZ)).T
    overlap = jnp.minimum(jnp.broadcast_to(after, (KZ, KZ)), wide)
    jumps = [jnp.concatenate([got[k, i * KD : (i + 1) * KD, :] for k in at], axis=0) for i in range(2)]
    jumps = jnp.concatenate(jumps, axis=1)
    later, behind = [], []
    for i in range(2):
        total = jnp.zeros((1, 128), F32)
        part = [None] * NZ
        for z in range(NZ - 1, -1, -1):
            part[z] = got[at[z], (2 + i) * KD : (3 + i) * KD, :] + total
            total = total + got[at[z], 4 * KD + i : 4 * KD + i + 1, :]
        later.append(total)
        behind.append(jnp.concatenate(part, axis=0))
    later = jnp.concatenate(later, axis=1)
    own = jnp.dot(overlap, jumps, precision=lax.Precision.HIGHEST, preferred_element_type=F32)
    corr = jnp.concatenate(behind, axis=1) - own
    small[TOTAL : TOTAL + 1, :] = later
    small[JUMPS : JUMPS + 1, :] = column_sum(jumps)
    small[WEIGHTED : WEIGHTED + 1, :] = column_sum(jumps * wide)
    small[AFTER : AFTER + 1, :] = after
    small[CORR : CORR + 1, :] = column_sum(corr)
    small[CORR + 1 :, :] = jnp.zeros((7 - CORR, KZ), F32)
    big[0:KZ, :] = jumps.T
    big[KZ:, :] = corr.T


def places():
    x = lax.axis_index("x")
    return [lax.rem(x + NX - k, NX) for k in range(NX)]


def turn_x(k):
    return lax.rem(k + 1, NX)


def weights(place):
    one = lambda c: jnp.where(c, 1.0, 0.0).astype(F32)
    return [[one(place[q] < place[p]) for q in range(NX)] for p in range(NX)]


def weigh(before, p, values, later=False):
    out = 0.0
    for q in range(NX):
        if q != p:
            out = out + (before[q][p] if later else before[p][q]) * values[q]
    return out


def base_rows(before, smalls):
    row = lambda p, k: smalls[p][k : k + 1, :]
    lower = [weigh(before, p, [row(q, JUMPS) for q in range(NX)]) for p in range(NX)]
    upper = [weigh(before, p, [row(q, TOTAL) - row(q, WEIGHTED) for q in range(NX)], True) for p in range(NX)]
    return lower, upper


def own_stats(big, ms, stats):
    place = places()
    smalls = [ms.at[turn_x(k)] for k in place]
    m0 = smalls[0]
    before = weights(place)
    lower, upper = base_rows(before, smalls)
    after = m0[AFTER : AFTER + 1, :]
    columns = jnp.concatenate([lower[0], upper[0]] + [jnp.zeros((6, KZ), F32)], axis=0).T
    jumps = big[0:KZ, :]
    corr = big[KZ:, :] + columns[:, 1:2] - columns[:, 0:1] * after
    sums = []
    for p in range(NX):
        reach = jnp.sum(smalls[p][AFTER : AFTER + 1, :], axis=1, keepdims=True)
        sums.append(smalls[p][CORR : CORR + 1, :] + float(KZ) * upper[p] - reach * lower[p])
    lead = weigh(before, 0, sums)
    weighted = jnp.sum(corr * after, axis=1, keepdims=True)
    cross = 2.0 * jnp.sum(weighted * jnp.broadcast_to(lead, (8, KZ)).T[:, 0:1])
    curv = column_sum(corr * times_overlap(corr, gram(after)))
    lane = lax.broadcasted_iota(jnp.int32, (1, KZ), 1)
    stats[0:1, :] = column_sum(jumps * jumps)
    stats[1:2, :] = column_sum(jumps * corr)
    stats[2:3, :] = column_sum(corr * corr)
    stats[3:4, :] = curv + jnp.where(lane == 0, cross, 0.0)
    stats[4:, :] = jnp.zeros((4, KZ), F32)


def shrink_of(rows):
    grad, curv = rows(0, 2), rows(0, 3)
    for p in range(1, NX):
        grad, curv = grad + rows(p, 2), curv + rows(p, 3)
    step = jnp.sum(grad, axis=1, keepdims=True) / (jnp.sum(curv, axis=1, keepdims=True) + EPS)
    norms, level = [], 0.0
    for p in range(NX):
        square = rows(p, 0) + 2.0 * step * rows(p, 1) + step * step * rows(p, 2)
        norms.append(jnp.sqrt(jnp.maximum(square, 0.0) + EPS))
        level = level + norms[-1]
    level = jnp.sum(level, axis=1, keepdims=True) / (NX * KZ)
    return step, [jnp.maximum(0.0, 1.0 - SHRINK * level / n) for n in norms]


def second_corr(b0, b1, b2, b3, ms, ss, jumps_out, corr_out, stats):
    place = places()
    smalls = [ms.at[turn_x(k)] for k in place]
    bigs, sums_in = (b0, b1, b2, b3), [ss.at[turn_x(k)] for k in place]
    before = weights(place)
    after = [m[AFTER : AFTER + 1, :] for m in smalls]
    overlap = [gram(a) for a in after]
    lower, upper = base_rows(before, smalls)
    columns = jnp.concatenate(lower + upper, axis=0).T
    step, factor = shrink_of(lambda p, k: sums_in[p][k : k + 1, :])
    jumps, corr, change, sums, weighted = [], [], [], [], []
    for p in range(NX):
        j = bigs[p][0:KZ, :]
        c = bigs[p][KZ:, :] + columns[:, NX + p : NX + p + 1] - columns[:, p : p + 1] * after[p]
        new = factor[p] * (j + step * c)
        d = new - j
        jumps_out[p] = new
        jumps.append(new)
        corr.append(c)
        change.append(d)
        sums.append(jnp.sum(d, axis=1, keepdims=True))
        weighted.append(jnp.sum(d * after[p], axis=1, keepdims=True))
    for p in range(NX):
        low, high = weigh(before, p, sums), weigh(before, p, weighted, True)
        corr[p] = corr[p] - times_overlap(change[p], overlap[p]) - low * after[p] - high
        corr_out[p] = corr[p]
    curv = jnp.zeros((1, KZ), F32)
    for p in range(NX):
        c, j = corr[p], jumps[p]
        sums[p] = jnp.sum(c, axis=1, keepdims=True)
        weighted[p] = jnp.sum(c * after[p], axis=1, keepdims=True)
        stats[4 * p : 4 * p + 1, :] = column_sum(j * j)
        stats[4 * p + 1 : 4 * p + 2, :] = column_sum(j * c)
        stats[4 * p + 2 : 4 * p + 3, :] = column_sum(c * c)
        curv += column_sum(c * times_overlap(c, overlap[p]))
    cross = jnp.zeros((KZ, 1), F32)
    for p in range(NX):
        cross += weighted[p] * weigh(before, p, sums)
    lane = lax.broadcasted_iota(jnp.int32, (1, KZ), 1)
    stats[3:4, :] = curv + jnp.where(lane == 0, 2.0 * jnp.sum(cross), 0.0)
    for p in range(1, NX):
        stats[4 * p + 3 : 4 * p + 4, :] = jnp.zeros((1, KZ), F32)


def finish(bins, signal, m0, jumps_in, corr_in, s0, s1, s2, s3, resid, jumps_out, held, sems):
    before = weights(places())[0]
    x, z = lax.axis_index("x"), lax.axis_index("z")
    width = signal.shape[1]
    total = (s0[...] + s1[...]) + (s2[...] + s3[...])
    step, factor = shrink_of(lambda p, k: total[4 * p + k : 4 * p + k + 1, :])
    left = jnp.zeros((KZ, KZ), F32)
    for p in range(1, NX):
        left += (before[p] * factor[p]) * (jumps_in[p] + step * corr_in[p])
    left = jnp.sum(left, axis=1, keepdims=True)
    new = factor[0] * (jumps_in[0] + step * corr_in[0])
    marks = (bins - 1.0) - m0[AFTER : AFTER + 1, :]
    wide = jnp.broadcast_to(marks, (KZ, KZ)).T
    start = ((x * NZ + z) * width).astype(F32)
    part = pieces(new)
    copies = []
    for i in range(width // CHUNK):
        bin_at = lax.broadcasted_iota(jnp.int32, (KZ, CHUNK), 1).astype(F32) + (start + i * CHUNK)
        mask = (wide < bin_at).astype(BF16)
        fit = jnp.zeros((KZ, CHUNK), F32)
        for piece in part[::-1]:
            fit += mul(piece, mask)
        here = slice(i * CHUNK, (i + 1) * CHUNK)
        held[:, here] = signal[:, here] - (fit + left)
        copies.append(pltpu.make_async_copy(held.at[:, here], resid.at[:, here], sems.at[i]))
        copies[-1].start()
    jumps_out[...] = pltpu.roll(new, lax.rem(KZ - z * KD, KZ), 1)[:, :128].T[:KD]
    for copy in copies:
        copy.wait()


def round_x(block):
    ring = lambda k: [(i, (i + k) % NX) for i in range(NX)]
    return [block] + [lax.ppermute(block, "x", ring(k)) for k in range(1, NX)]


def over_samples(stats):
    stats = stats + lax.ppermute(stats, "core", [(0, 1), (1, 0)])
    return [stats] + [lax.ppermute(stats, "y", [(i, i ^ k) for i in range(NY)]) for k in (1, 2, 3)]


def body(signal, jumps, breaks):
    rows, width = signal.shape
    bins = float(width * NX * NZ)
    slab = [pltpu.VMEM((rows, width), F32), pltpu.SemaphoreType.DMA((width // CHUNK,))]
    first = call(
        local_sums,
        [(4 * KD + 8, rows // 2)],
        [HBM] * 3,
        scratch=[pltpu.SMEM((KD,), jnp.int32)] + slab + [pltpu.SemaphoreType.DMA((3,))],
    )
    (mine,) = first(*[pltpu.with_memory_space_constraint(a, pltpu.HBM) for a in (breaks, signal, jumps.T)])
    near = lax.all_to_all(
        jnp.broadcast_to(mine[None], (NZ,) + mine.shape), "z", 0, 0, axis_index_groups=[TURN_Z], tiled=False
    )
    big, small = call(functools.partial(group_sums, bins), [(2 * KZ, rows), (8, rows)], [VMEM])(near)
    ring = lambda k: [(i, (i + k) % NX) for i in range(NX)]
    b1, b3 = lax.ppermute(big, "x", ring(1)), lax.ppermute(big, "x", ring(3))
    smalls = lax.all_to_all(
        jnp.broadcast_to(small[None], (NX,) + small.shape), "x", 0, 0, axis_index_groups=[TURN_X], tiled=False
    )
    (stats,) = call(own_stats, [(8, KZ)], [VMEM] * 2)(big, smalls)
    late, stats = lax.optimization_barrier((big, stats))
    bigs = [big, b1, lax.ppermute(late, "x", ring(2)), b3]
    stats = stats + lax.ppermute(stats, "core", [(0, 1), (1, 0)])
    stats = lax.all_to_all(jnp.broadcast_to(stats[None], (NY,) + stats.shape), "y", 0, 0, axis_index_groups=[TURN_Y], tiled=False).sum(0)
    sums = lax.all_to_all(
        jnp.broadcast_to(stats[None], (NX,) + stats.shape), "x", 0, 0, axis_index_groups=[TURN_X], tiled=False
    )
    jumps1, corr, stats = call(second_corr, [(NX, rows, KZ), (NX, rows, KZ), (16, KZ)], [VMEM] * 6)(*bigs, smalls, sums)
    parts = over_samples(stats)
    last = call(functools.partial(finish, bins), [(rows, width), (KD, rows)], [VMEM] * 8, [HBM, VMEM], slab)
    resid, jumps2 = last(signal, small, jumps1, corr, *parts)
    return resid, jumps2.T


def solution(mesh):
    fine = Mesh(mesh.devices.reshape(NX, NZ, NY, NC), ("x", "z", "y", "core"))
    both = P(("y", "core"), ("x", "z"))
    return jax.shard_map(
        body,
        mesh=fine,
        in_specs=(both, both, P(("x", "z"))),
        out_specs=(both, both),
        check_vma=False,
    )
```
